256 devices in a mesh: fsdp: 32 (over x, y, core), grp: 8 (over z).
Axes of the slice: x: 4, y: 4, z: 8, core: 2. Of those that a mesh axis runs over, the one named last changes fastest.
Arguments:
- grad: bfloat16 [16, 512, 7168], P(None, ('fsdp', 'grp')), may hold values from -6 to 6
- owner: int32 [224], replicated, may hold values from 0 to 511, as said below
- refresh: int32 [224], replicated, may hold values from 0 to 1, as said below
- stats_left: float32 [512, 512, 512], P(('fsdp', 'grp'))
- stats_right: float32 [512, 512, 512], P(('fsdp', 'grp'))
- old_roots: bfloat16 [512, 2, 512, 512], P(('fsdp', 'grp'))
- fresh_roots: bfloat16 [256, 2, 512, 512], P(('fsdp', 'grp'))
Outputs:
- new_left: float32 [512, 512, 512], P(('fsdp', 'grp'))
- new_right: float32 [512, 512, 512], P(('fsdp', 'grp'))
- update: bfloat16 [16, 512, 7168], P(None, ('fsdp', 'grp'))
The draws below stay inside these ranges and needn't reach their ends.
Inputs may be any that keep to these rules, and one draw needn't show every extreme that they name: `owner`: no two blocks share a slot. Some device has all its 2 slots taken. `refresh`: of the blocks on one device at most one has 1; some block has 1.
All inputs are finite; a program needn't handle non-finite values.
Results may differ from the reference program's by a relative error of at most 0.0049.
Values may be sent and summed in bfloat16 or wider, within the bound.
A program may use at most 64 MiB of HBM per device.

```python
import jax
import jax.numpy as jnp
from jax import lax

D = 7168
B = 512
RB = 1
CAP = 2
MATS = 16
N_GRP = 8
DEVICES = 256


def placement(key):
    key_slots = jax.random.fold_in(key, 101)
    key_blocks = jax.random.fold_in(key, 102)
    key_pick = jax.random.fold_in(key, 103)
    slot_total = CAP * DEVICES
    block_total = MATS * RB * (D // B)
    slots = jax.random.permutation(key_slots, slot_total).astype(jnp.int32)
    full_device = slots[0] // CAP
    position = jnp.arange(slot_total, dtype=jnp.int32)
    scores = jnp.where(slots // CAP == full_device, slots % CAP - CAP, position)
    ordered = slots[jnp.argsort(scores, stable=True)]
    blocks = jax.random.permutation(key_blocks, block_total).astype(jnp.int32)
    owner = jnp.zeros((block_total,), jnp.int32).at[blocks].set(ordered[:block_total])
    picks = jax.random.randint(key_pick, (DEVICES,), 0, CAP + 1).astype(jnp.int32)
    picks = picks.at[full_device].set(0)
    refresh = (owner % CAP == picks[owner // CAP]).astype(jnp.int32)
    return (owner, refresh)


def symmetric_draw(key, count, lower, upper, offdiag, noise):
    diagonal = jnp.exp(jax.random.uniform(key, (count, 1, B), jnp.float32, jnp.log(lower), jnp.log(upper)))
    mirrored = (noise + jnp.swapaxes(noise, 1, 2)) * (offdiag / jnp.sqrt(2.0 * B))
    identity = (jnp.arange(B)[:, None] == jnp.arange(B)[None, :]).astype(jnp.float32)
    return diagonal * identity + mirrored * (1.0 - identity)


def noise_draw(key, shape):
    return jax.random.normal(key, shape, jnp.float32)


def draw_owner(key, part):
    shared = placement(key)
    return shared[0]


def draw_refresh(key, part):
    shared = placement(key)
    return shared[1]


def draw_stats_left(key, part):
    key = jax.random.fold_in(key, 3)
    first, second = jax.random.split(key)
    count = CAP * DEVICES
    return symmetric_draw(first, count, 0.5, 5.0, 0.8, noise_draw(second, (count, B, B)))


def draw_stats_right(key, part):
    key = jax.random.fold_in(key, 4)
    first, second = jax.random.split(key)
    count = CAP * DEVICES
    return symmetric_draw(first, count, 0.5, 5.0, 0.8, noise_draw(second, (count, B, B)))


def draw_old_roots(key, part):
    key = jax.random.fold_in(key, 5)
    first, second = jax.random.split(key)
    count = CAP * DEVICES * 2
    matrices = symmetric_draw(first, count, 0.3, 3.0, 0.8, noise_draw(second, (count, B, B)))
    return matrices.reshape(CAP * DEVICES, 2, B, B).astype(jnp.bfloat16)


def draw_fresh_roots(key, part):
    key = jax.random.fold_in(key, 6)
    first, second = jax.random.split(key)
    count = DEVICES * 2
    matrices = symmetric_draw(first, count, 0.3, 3.0, 0.8, noise_draw(second, (count, B, B)))
    return matrices.reshape(DEVICES, 2, B, B).astype(jnp.bfloat16)


def block_levels(key, shape, cuts, least, largest):
    loudness = 1.0
    for dim, blocks in cuts:
        draws = jax.random.uniform(jax.random.fold_in(jax.random.fold_in(key, 6), dim), (blocks,), jnp.float32, least / len(cuts), largest / len(cuts))
        loudness = loudness * jnp.repeat(jnp.exp(draws), shape[dim] // blocks).reshape((-1,) + (1,) * (len(shape) - 1 - dim))
    return loudness


def scatter_about(rng, shape, width, most, shards=(), kind=jnp.bfloat16):
    values = width * jax.random.normal(rng, shape, jnp.float32)
    if shards:
        values = values * block_levels(rng, shape, shards, -0.22, 0.18)
    return jnp.clip(values, -most, most).astype(kind)


def setup_inputs(seed: int = 0) -> dict:
    keys = jax.random.split(jax.random.key(seed), 8)
    return {
        "grad": scatter_about(keys[0], (MATS, RB * B, D), 1.0, 6.0, ((1, 256),)),
        "owner": draw_owner(jax.random.fold_in(keys[7], 71), 0),
        "refresh": draw_refresh(jax.random.fold_in(keys[7], 71), 0),
        "stats_left": draw_stats_left(jax.random.fold_in(keys[7], 71), 0),
        "stats_right": draw_stats_right(jax.random.fold_in(keys[7], 71), 0),
        "old_roots": draw_old_roots(jax.random.fold_in(keys[7], 71), 0),
        "fresh_roots": draw_fresh_roots(jax.random.fold_in(keys[7], 71), 0),
    }


decay_rate = 0.999
epsilon = 1e-06

def reference(grad, owner, refresh, stats_left, stats_right, old_roots, fresh_roots):
    block_cols = D // B
    block_total = MATS * RB * block_cols
    pieces = grad.reshape(MATS, RB, B, block_cols, B).transpose(0, 1, 3, 2, 4).reshape(block_total, B, B)

    def one_block(index):
        slot = owner[index]
        device = slot // CAP
        fsdp_index = device // N_GRP
        grp_index = device % N_GRP
        source = fsdp_index * N_GRP + (grp_index + N_GRP - 1) % N_GRP
        piece = pieces[index]
        inverse_roots = jnp.where(refresh[index] == 1, fresh_roots[source], old_roots[slot])
        left = decay_rate * stats_left[slot] + (1.0 - decay_rate) * jnp.dot(piece, piece.T, preferred_element_type=jnp.float32)
        right = decay_rate * stats_right[slot] + (1.0 - decay_rate) * jnp.dot(piece.T, piece, preferred_element_type=jnp.float32)
        left_applied = jnp.dot(inverse_roots[0], piece, preferred_element_type=jnp.float32).astype(jnp.bfloat16)
        shaped = jnp.dot(left_applied, inverse_roots[1], preferred_element_type=jnp.float32)
        wide = piece.astype(jnp.float32)
        graft_scale = jnp.sqrt(jnp.mean(wide * wide) + epsilon) / jnp.sqrt(jnp.mean(shaped * shaped) + epsilon)
        return (left, right, (shaped * graft_scale).astype(jnp.bfloat16))
    lefts, rights, updates = lax.map(one_block, jnp.arange(block_total, dtype=jnp.int32))
    new_left = stats_left.at[owner].set(lefts)
    new_right = stats_right.at[owner].set(rights)
    update = updates.reshape(MATS, RB, block_cols, B, B).transpose(0, 1, 3, 2, 4).reshape(MATS, RB * B, D)
    return (new_left, new_right, update)
```

```python
import functools

import jax
import jax.numpy as jnp
from jax import lax
from jax.experimental import pallas as pl
from jax.experimental.pallas import tpu as pltpu
from jax.sharding import PartitionSpec as P

decay_rate = 0.999
epsilon = 1e-06

CHUNKS = 4
IN_CAP = 56
OUT_CAP = 48
ROLES = 3

MESH = pl.DeviceIdType.MESH


def shifted(block, axis, distance):
    devices = range(lax.axis_size(axis))
    route = [((i - distance) % len(devices), i) for i in devices]
    return lax.ppermute(block, axis, route)


def slot_work(piece, left, right, inverse_roots):
    new_left = decay_rate * left + (1.0 - decay_rate) * jnp.dot(
        piece, piece.T, preferred_element_type=jnp.float32
    )
    new_right = decay_rate * right + (1.0 - decay_rate) * jnp.dot(
        piece.T, piece, preferred_element_type=jnp.float32
    )
    left_applied = jnp.dot(inverse_roots[0], piece, preferred_element_type=jnp.float32).astype(
        jnp.bfloat16
    )
    shaped = jnp.dot(left_applied, inverse_roots[1], preferred_element_type=jnp.float32)
    wide = piece.astype(jnp.float32)
    graft_scale = jnp.sqrt(jnp.mean(wide * wide) + epsilon) / jnp.sqrt(
        jnp.mean(shaped * shaped) + epsilon
    )
    return (new_left, new_right, (shaped * graft_scale).astype(jnp.bfloat16))


def dense_plan(grad, owner, refresh, stats_left, stats_right, old_roots, fresh_roots):
    matrices, row_count, width = grad.shape
    capacity, block_size = (stats_left.shape[0], stats_left.shape[1])
    block_cols = width // block_size
    fsdp_count = lax.axis_size("fsdp")
    grp_count = lax.axis_size("grp")
    device_total = fsdp_count * grp_count
    row_blocks = row_count * device_total // block_size
    block_total = matrices * row_blocks * block_cols
    self_index = lax.axis_index("fsdp") * grp_count + lax.axis_index("grp")
    my_row = self_index // (device_total // row_blocks)
    local_blocks = grad.reshape(matrices, row_count, block_cols, block_size).transpose(0, 2, 1, 3)
    local_blocks = local_blocks.reshape(matrices * block_cols, row_count, block_size)
    slot_ids = jnp.arange(capacity, dtype=jnp.int32)[:, None, None]
    fsdp_ids = jnp.arange(fsdp_count, dtype=jnp.int32)[None, :, None]
    grp_ids = jnp.arange(grp_count, dtype=jnp.int32)[None, None, :]
    slot_order = ((fsdp_ids * grp_count + grp_ids) * capacity + slot_ids).reshape(-1)
    block_ids = jnp.arange(block_total, dtype=jnp.int32)
    matches = owner[None, :] == slot_order[:, None]
    present = jnp.any(matches, axis=1)
    chosen_block = jnp.sum(jnp.where(matches, block_ids[None, :], 0), axis=1)
    chosen_row = chosen_block // block_cols % row_blocks
    local_index = chosen_block // (row_blocks * block_cols) * block_cols + chosen_block % block_cols
    sending = present & (chosen_row == my_row)
    outbound = jnp.where(
        sending[:, None, None], local_blocks[local_index], jnp.zeros((), jnp.bfloat16)
    )
    outbound = outbound.reshape(capacity, fsdp_count, grp_count, row_count, block_size)
    inbound = lax.all_to_all(
        lax.all_to_all(outbound, "fsdp", split_axis=1, concat_axis=1, tiled=True),
        "grp",
        split_axis=2,
        concat_axis=2,
        tiled=True,
    )
    own_slots = self_index * capacity + jnp.arange(capacity, dtype=jnp.int32)
    own_matches = owner[None, :] == own_slots[:, None]
    occupied = jnp.any(own_matches, axis=1)
    own_block = jnp.sum(jnp.where(own_matches, block_ids[None, :], 0), axis=1)
    own_row = own_block // block_cols % row_blocks
    row_pick = (jnp.arange(row_blocks, dtype=jnp.int32)[None, :] == own_row[:, None])[
        :, :, None, None
    ]
    stacked = inbound.reshape(capacity, row_blocks, block_size, block_size)
    pieces = jnp.sum(jnp.where(row_pick, stacked, jnp.zeros((), jnp.bfloat16)), axis=1)
    renewal = jnp.sum(jnp.where(own_matches, refresh[None, :], 0), axis=1) == 1
    renewed = shifted(fresh_roots, "grp", 1)[0]
    inverse_roots = jnp.where(renewal[:, None, None, None], renewed[None], old_roots)
    lefts, rights, slot_update = jax.vmap(slot_work)(pieces, stats_left, stats_right, inverse_roots)
    new_left = jnp.where(occupied[:, None, None], lefts, stats_left)
    new_right = jnp.where(occupied[:, None, None], rights, stats_right)
    placed = jnp.where(row_pick, slot_update[:, None], jnp.zeros((), jnp.bfloat16))
    outgoing = placed.reshape(capacity, fsdp_count, grp_count, row_count, block_size)
    returned = lax.all_to_all(
        lax.all_to_all(outgoing, "fsdp", split_axis=1, concat_axis=1, tiled=True),
        "grp",
        split_axis=2,
        concat_axis=2,
        tiled=True,
    )
    returned = returned.reshape(capacity * device_total, row_count, block_size)
    matrix_ids = jnp.arange(matrices, dtype=jnp.int32)[:, None]
    column_ids = jnp.arange(block_cols, dtype=jnp.int32)[None, :]
    wanted = ((matrix_ids * row_blocks + my_row) * block_cols + column_ids).reshape(-1)
    wanted_owner = owner[wanted]
    position = wanted_owner % capacity * device_total + wanted_owner // capacity
    gathered = returned[position].reshape(matrices, block_cols, row_count, block_size)
    update = gathered.transpose(0, 2, 1, 3).reshape(matrices, row_count, width)
    return (new_left, new_right, update)


def make_tables(owner, refresh, fsdp_count, grp_count, capacity, block_cols):
    my_grp = lax.axis_index("grp")
    my_device = lax.axis_index("fsdp") * grp_count + my_grp
    plane_size = fsdp_count * ROLES
    blocks = jnp.arange(owner.shape[0], dtype=jnp.int32)
    device, slot = owner // capacity, owner % capacity
    column, plane = device // grp_count, device % grp_count
    renewed = refresh == 1
    root_plane = (plane + grp_count - 1) % grp_count
    own_role = plane * plane_size + column * ROLES + slot
    root_role = root_plane * plane_size + column * ROLES + capacity
    role = jnp.concatenate([own_role, jnp.where(renewed, root_role, -1)])
    to_plane = jnp.where(role >= 0, role // plane_size, -1)
    block = jnp.concatenate([blocks, blocks])
    position = jnp.sum(
        (to_plane[:, None] == to_plane[None, :]) & (role[:, None] < role[None, :]), axis=0, dtype=jnp.int32
    )
    flat = jnp.where(role >= 0, to_plane * IN_CAP + position, -1)
    block = block % block_cols * (owner.shape[0] // block_cols) + block // block_cols
    entry = jnp.arange(grp_count * IN_CAP, dtype=jnp.int32)
    send_block = jnp.sum(jnp.where(flat[None, :] == entry[:, None], block[None, :], 0), axis=1)
    mine = my_grp * plane_size + jnp.arange(plane_size, dtype=jnp.int32)
    take = jnp.sum(jnp.where(role[None, :] == mine[:, None], position[None, :], 0), axis=1)
    out_role = jnp.where(renewed, root_role, own_role)
    out_plane = out_role // plane_size
    out_position = jnp.sum(
        (out_plane[:, None] == out_plane[None, :]) & (out_role[:, None] < out_role[None, :]),
        axis=0,
        dtype=jnp.int32,
    )
    place = out_plane * OUT_CAP + out_position
    my_entry = my_grp * OUT_CAP + jnp.arange(OUT_CAP, dtype=jnp.int32)
    send_role = jnp.sum(
        jnp.where(place[None, :] == my_entry[:, None], (out_role - out_plane * plane_size)[None, :], 0), axis=1
    )
    fits = (jnp.max(jnp.where(role >= 0, position, 0)) < IN_CAP) & (jnp.max(out_position) < OUT_CAP)
    slots = my_device * capacity + jnp.arange(capacity, dtype=jnp.int32)
    held = jnp.any(owner[None, :] == slots[:, None], axis=1)
    keep = jnp.where(held, jnp.float32(decay_rate), jnp.float32(1.0))
    add = jnp.where(held, jnp.float32(1.0 - decay_rate), jnp.float32(0.0))
    return fits, send_block, take, send_role, place, jnp.concatenate([keep, add])


def step_kernel(
    sizes,
    send_block,
    take,
    send_role,
    place,
    factors,
    grad_hbm,
    left_hbm,
    right_hbm,
    old_hbm,
    fresh_hbm,
    new_left_hbm,
    new_right_hbm,
    update,
    grad,
    out1,
    in1,
    out2,
    pieces,
    shaped,
    in3,
    out4,
    in4,
    roots,
    left,
    right,
    local_sem,
    self_sem,
    send_sem,
    recv_sem,
):
    fsdp_count, grp_count, capacity, rows, block, block_cols, matrices = sizes
    plane_rows = grp_count * rows
    width = block // CHUNKS
    f, g = lax.axis_index("fsdp"), lax.axis_index("grp")

    def along(k):
        return lax.rem(g + k, grp_count)

    def across(k):
        return lax.rem(f + k, fsdp_count)

    loads = [
        pltpu.make_async_copy(
            grad_hbm.at[:, :, pl.ds(j * block, block)],
            grad.at[pl.ds(j * matrices, matrices)],
            local_sem.at[0],
        )
        for j in range(block_cols)
    ] + [
        pltpu.make_async_copy(old_hbm, roots.at[pl.ds(0, capacity)], local_sem.at[1]),
        pltpu.make_async_copy(fresh_hbm, roots.at[pl.ds(capacity, 1)], local_sem.at[2]),
        pltpu.make_async_copy(left_hbm, left, local_sem.at[3]),
        pltpu.make_async_copy(right_hbm, right, local_sem.at[4]),
    ]
    for load in loads:
        load.start()

    barrier = pltpu.get_barrier_semaphore()

    @pl.loop(1, grp_count)
    def _(k):
        pl.semaphore_signal(barrier, 1, device_id=(f, along(k)), device_id_type=MESH)

    @pl.loop(1, fsdp_count)
    def _(k):
        pl.semaphore_signal(barrier, 1, device_id=(across(k), g), device_id_type=MESH)

    pltpu.make_async_copy(grad, grad, local_sem.at[0]).wait()

    def gather_rows(chunks):
        @pl.loop(0, grp_count)
        def _(to):
            @pl.loop(0, IN_CAP, unroll=8)
            def _(i):
                both = grad[send_block[to * IN_CAP + i]]
                for c in chunks:
                    out1[c, to, i] = both[:, c * width : (c + 1) * width]

    def grp_copy(c, source, target, k, length, phase):
        return pltpu.make_async_remote_copy(
            src_ref=source.at[c, along(k)],
            dst_ref=target[c].at[pl.ds(g * length, length)],
            send_sem=send_sem.at[phase, c],
            recv_sem=recv_sem.at[phase, c],
            device_id=(f, along(k)),
            device_id_type=MESH,
        )

    def grp_wait(c, source, target, length, phase):
        everything = pltpu.make_async_remote_copy(
            src_ref=source.at[c, pl.ds(0, grp_count - 1)],
            dst_ref=target[c].at[pl.ds(0, (grp_count - 1) * length)],
            send_sem=send_sem.at[phase, c],
            recv_sem=recv_sem.at[phase, c],
            device_id=(f, g),
            device_id_type=MESH,
        )
        everything.wait_send()
        everything.wait_recv()

    def send_rows(c):
        pltpu.make_async_copy(out1.at[c, g], in1[c].at[pl.ds(g * IN_CAP, IN_CAP)], self_sem.at[0, c]).start()

        @pl.loop(1, grp_count)
        def _(k):
            grp_copy(c, out1, in1, k, IN_CAP, 0).start()

    gather_rows([0])
    pl.semaphore_wait(barrier, grp_count - 1 + fsdp_count - 1)
    send_rows(0)

    gather_rows(range(1, CHUNKS))
    for c in range(1, CHUNKS):
        send_rows(c)

    def spread(c):
        pltpu.make_async_copy(out1.at[c, g], in1[c].at[pl.ds(g * IN_CAP, IN_CAP)], self_sem.at[0, c]).wait()
        grp_wait(c, out1, in1, IN_CAP, 0)
        lanes = pl.ds(c * width, width)

        @pl.loop(0, fsdp_count)
        def _(k):
            to = across(k)
            for role in range(ROLES):
                i = take[to * ROLES + role]
                parts = [in1[c][source * IN_CAP + i] for source in range(grp_count)]
                out2[c, to * ROLES + role] = jnp.concatenate(parts, axis=0)

            source = out2.at[c, pl.ds(to * ROLES, ROLES)]
            target = pieces.at[:, pl.ds(pl.multiple_of(f * plane_rows, 16), plane_rows), lanes]

            @pl.when(k == 0)
            def _():
                pltpu.make_async_copy(source, target, self_sem.at[1, c]).start()

            @pl.when(k > 0)
            def _():
                pltpu.make_async_remote_copy(
                    src_ref=source,
                    dst_ref=target,
                    send_sem=send_sem.at[1, c],
                    recv_sem=recv_sem.at[1, c],
                    device_id=(to, g),
                    device_id_type=MESH,
                ).start()

    for c in range(CHUNKS):
        spread(c)

    def plane_wait(c, buffer, phase):
        everything = pltpu.make_async_remote_copy(
            src_ref=buffer.at[pl.ds(0, (fsdp_count - 1) * ROLES)],
            dst_ref=buffer.at[pl.ds(0, (fsdp_count - 1) * ROLES)],
            send_sem=send_sem.at[phase, c],
            recv_sem=recv_sem.at[phase, c],
            device_id=(f, g),
            device_id_type=MESH,
        )
        everything.wait_send()
        everything.wait_recv()

    for c in range(CHUNKS):
        own = out2.at[c, pl.ds(0, ROLES)]
        pltpu.make_async_copy(own, own, self_sem.at[1, c]).wait()
        plane_wait(c, out2.at[c], 1)

    loads[-4].wait()
    loads[-3].wait()

    @pl.loop(0, ROLES)
    def _(role):
        piece = pieces[role]
        applied = jnp.dot(roots[role, 0], piece, preferred_element_type=jnp.float32).astype(jnp.bfloat16)
        product = jnp.dot(applied, roots[role, 1], preferred_element_type=jnp.float32)
        wide = piece.astype(jnp.float32)
        count = 1.0 / (block * block)
        scale = jnp.sqrt(jnp.sum(wide * wide, keepdims=True) * count + epsilon) * lax.rsqrt(
            jnp.sum(product * product, keepdims=True) * count + epsilon
        )
        shaped[role] = (product * scale).astype(jnp.bfloat16)

    def send_back(c):
        lanes = pl.ds(c * width, width)

        @pl.loop(0, fsdp_count)
        def _(k):
            to = across(k)
            source = shaped.at[:, pl.ds(pl.multiple_of(to * plane_rows, 16), plane_rows), lanes]
            target = in3[c].at[pl.ds(f * ROLES, ROLES)]

            @pl.when(k == 0)
            def _():
                pltpu.make_async_copy(source, target, self_sem.at[2, c]).start()

            @pl.when(k > 0)
            def _():
                pltpu.make_async_remote_copy(
                    src_ref=source,
                    dst_ref=target,
                    send_sem=send_sem.at[2, c],
                    recv_sem=recv_sem.at[2, c],
                    device_id=(to, g),
                    device_id_type=MESH,
                ).start()

    for c in range(CHUNKS):
        send_back(c)

    loads[-2].wait()
    loads[-1].wait()

    @pl.loop(0, capacity)
    def _(slot):
        piece = pieces[slot]
        keep, add = factors[slot], factors[capacity + slot]
        outer = lax.dot_general(piece, piece, (((1,), (1,)), ((), ())), preferred_element_type=jnp.float32)
        left[slot] = keep * left[slot] + add * outer
        inner = lax.dot_general(piece, piece, (((0,), (0,)), ((), ())), preferred_element_type=jnp.float32)
        right[slot] = keep * right[slot] + add * inner

    stores = [
        pltpu.make_async_copy(left, new_left_hbm, local_sem.at[5]),
        pltpu.make_async_copy(right, new_right_hbm, local_sem.at[6]),
    ]
    for store in stores:
        store.start()

    for c in range(CHUNKS):
        own = in3[c].at[pl.ds(0, ROLES)]
        pltpu.make_async_copy(own, own, self_sem.at[2, c]).wait()
        plane_wait(c, in3[c], 2)

        @pl.loop(0, OUT_CAP, unroll=2)
        def _(i):
            tile = in3[c][send_role[i]]
            for to in range(grp_count):
                out4[c, to, i] = tile[to * rows : (to + 1) * rows]

        pltpu.make_async_copy(out4.at[c, g], in4[c].at[pl.ds(g * OUT_CAP, OUT_CAP)], self_sem.at[3, c]).start()

        @pl.loop(1, grp_count)
        def _(k):
            grp_copy(c, out4, in4, k, OUT_CAP, 3).start()

    for c in range(CHUNKS):
        pltpu.make_async_copy(out4.at[c, g], in4[c].at[pl.ds(g * OUT_CAP, OUT_CAP)], self_sem.at[3, c]).wait()
        grp_wait(c, out4, in4, OUT_CAP, 3)

        @pl.loop(0, matrices)
        def _(m):
            for j in range(block_cols):
                column = j * block + c * width
                update[m, :, pl.ds(column, width)] = in4[c][place[m * block_cols + j]]

    for store in stores:
        store.wait()


def listed_plan(tables, grad, stats_left, stats_right, old_roots, fresh_roots):
    matrices, rows, total_width = grad.shape
    capacity, block = stats_left.shape[0], stats_left.shape[1]
    fsdp_count, grp_count = lax.axis_size("fsdp"), lax.axis_size("grp")
    sizes = (fsdp_count, grp_count, capacity, rows, block, total_width // block, matrices)
    width, plane_rows = block // CHUNKS, grp_count * rows
    bf16 = jnp.bfloat16
    smem, hbm = pl.BlockSpec(memory_space=pltpu.SMEM), pl.BlockSpec(memory_space=pl.ANY)
    return pl.pallas_call(
        functools.partial(step_kernel, sizes),
        out_shape=(
            jax.ShapeDtypeStruct(stats_left.shape, jnp.float32),
            jax.ShapeDtypeStruct(stats_right.shape, jnp.float32),
            jax.ShapeDtypeStruct(grad.shape, bf16),
        ),
        in_specs=[smem] * 5 + [hbm] * 5,
        out_specs=(hbm, hbm, pl.BlockSpec(memory_space=pltpu.VMEM)),
        scratch_shapes=[
            pltpu.VMEM((matrices * (total_width // block), rows, block), bf16),
            pltpu.VMEM((CHUNKS, grp_count, IN_CAP, rows, width), bf16),
            [pltpu.VMEM((grp_count * IN_CAP, rows, width), bf16)] * CHUNKS,
            pltpu.VMEM((CHUNKS, fsdp_count * ROLES, plane_rows, width), bf16),
            pltpu.VMEM((ROLES, block, block), bf16),
            pltpu.VMEM((ROLES, block, block), bf16),
            [pltpu.VMEM((fsdp_count * ROLES, plane_rows, width), bf16)] * CHUNKS,
            pltpu.VMEM((CHUNKS, grp_count, OUT_CAP, rows, width), bf16),
            [pltpu.VMEM((grp_count * OUT_CAP, rows, width), bf16)] * CHUNKS,
            pltpu.VMEM((ROLES, 2, block, block), bf16),
            pltpu.VMEM(stats_left.shape, jnp.float32),
            pltpu.VMEM(stats_right.shape, jnp.float32),
            pltpu.SemaphoreType.DMA((7,)),
            pltpu.SemaphoreType.DMA((4, CHUNKS)),
            pltpu.SemaphoreType.DMA((4, CHUNKS)),
            pltpu.SemaphoreType.DMA((4, CHUNKS)),
        ],
        compiler_params=pltpu.CompilerParams(
            collective_id=1, has_side_effects=True, vmem_limit_bytes=48 * 1024 * 1024
        ),
        name="listed_step",
    )(*tables, grad, stats_left, stats_right, old_roots, fresh_roots)


def local(grad, owner, refresh, stats_left, stats_right, old_roots, fresh_roots):
    fits, *tables = make_tables(
        owner,
        refresh,
        lax.axis_size("fsdp"),
        lax.axis_size("grp"),
        stats_left.shape[0],
        grad.shape[2] // stats_left.shape[1],
    )
    return lax.cond(
        fits,
        lambda: listed_plan(tables, grad, stats_left, stats_right, old_roots, fresh_roots),
        lambda: dense_plan(grad, owner, refresh, stats_left, stats_right, old_roots, fresh_roots),
    )


def solution(mesh):
    return jax.shard_map(
        local,
        mesh=mesh,
        in_specs=(
            P(None, ("fsdp", "grp"), None),
            P(),
            P(),
            P(("fsdp", "grp"), None, None),
            P(("fsdp", "grp"), None, None),
            P(("fsdp", "grp"), None, None, None),
            P(("fsdp", "grp"), None, None, None),
        ),
        out_specs=(
            P(("fsdp", "grp"), None, None),
            P(("fsdp", "grp"), None, None),
            P(None, ("fsdp", "grp"), None),
        ),
        check_vma=False,
    )
```

```python
import functools

import jax
import jax.numpy as jnp
from jax import lax
from jax.experimental import pallas as pl
from jax.experimental.pallas import tpu as pltpu
from jax.sharding import PartitionSpec as P

decay_rate = 0.999
epsilon = 1e-06

CHUNKS = 4
IN_CAP = 52
OUT_CAP = 42
ROLES = 3

MESH = pl.DeviceIdType.MESH


def shifted(block, axis, distance):
    devices = range(lax.axis_size(axis))
    route = [((i - distance) % len(devices), i) for i in devices]
    return lax.ppermute(block, axis, route)


def slot_work(piece, left, right, inverse_roots):
    new_left = decay_rate * left + (1.0 - decay_rate) * jnp.dot(
        piece, piece.T, preferred_element_type=jnp.float32
    )
    new_right = decay_rate * right + (1.0 - decay_rate) * jnp.dot(
        piece.T, piece, preferred_element_type=jnp.float32
    )
    left_applied = jnp.dot(inverse_roots[0], piece, preferred_element_type=jnp.float32).astype(
        jnp.bfloat16
    )
    shaped = jnp.dot(left_applied, inverse_roots[1], preferred_element_type=jnp.float32)
    wide = piece.astype(jnp.float32)
    graft_scale = jnp.sqrt(jnp.mean(wide * wide) + epsilon) / jnp.sqrt(
        jnp.mean(shaped * shaped) + epsilon
    )
    return (new_left, new_right, (shaped * graft_scale).astype(jnp.bfloat16))


def dense_plan(grad, owner, refresh, stats_left, stats_right, old_roots, fresh_roots):
    matrices, row_count, width = grad.shape
    capacity, block_size = (stats_left.shape[0], stats_left.shape[1])
    block_cols = width // block_size
    fsdp_count = lax.axis_size("fsdp")
    grp_count = lax.axis_size("grp")
    device_total = fsdp_count * grp_count
    row_blocks = row_count * device_total // block_size
    block_total = matrices * row_blocks * block_cols
    self_index = lax.axis_index("fsdp") * grp_count + lax.axis_index("grp")
    my_row = self_index // (device_total // row_blocks)
    local_blocks = grad.reshape(matrices, row_count, block_cols, block_size).transpose(0, 2, 1, 3)
    local_blocks = local_blocks.reshape(matrices * block_cols, row_count, block_size)
    slot_ids = jnp.arange(capacity, dtype=jnp.int32)[:, None, None]
    fsdp_ids = jnp.arange(fsdp_count, dtype=jnp.int32)[None, :, None]
    grp_ids = jnp.arange(grp_count, dtype=jnp.int32)[None, None, :]
    slot_order = ((fsdp_ids * grp_count + grp_ids) * capacity + slot_ids).reshape(-1)
    block_ids = jnp.arange(block_total, dtype=jnp.int32)
    matches = owner[None, :] == slot_order[:, None]
    present = jnp.any(matches, axis=1)
    chosen_block = jnp.sum(jnp.where(matches, block_ids[None, :], 0), axis=1)
    chosen_row = chosen_block // block_cols % row_blocks
    local_index = chosen_block // (row_blocks * block_cols) * block_cols + chosen_block % block_cols
    sending = present & (chosen_row == my_row)
    outbound = jnp.where(
        sending[:, None, None], local_blocks[local_index], jnp.zeros((), jnp.bfloat16)
    )
    outbound = outbound.reshape(capacity, fsdp_count, grp_count, row_count, block_size)
    inbound = lax.all_to_all(
        lax.all_to_all(outbound, "fsdp", split_axis=1, concat_axis=1, tiled=True),
        "grp",
        split_axis=2,
        concat_axis=2,
        tiled=True,
    )
    own_slots = self_index * capacity + jnp.arange(capacity, dtype=jnp.int32)
    own_matches = owner[None, :] == own_slots[:, None]
    occupied = jnp.any(own_matches, axis=1)
    own_block = jnp.sum(jnp.where(own_matches, block_ids[None, :], 0), axis=1)
    own_row = own_block // block_cols % row_blocks
    row_pick = (jnp.arange(row_blocks, dtype=jnp.int32)[None, :] == own_row[:, None])[
        :, :, None, None
    ]
    stacked = inbound.reshape(capacity, row_blocks, block_size, block_size)
    pieces = jnp.sum(jnp.where(row_pick, stacked, jnp.zeros((), jnp.bfloat16)), axis=1)
    renewal = jnp.sum(jnp.where(own_matches, refresh[None, :], 0), axis=1) == 1
    renewed = shifted(fresh_roots, "grp", 1)[0]
    inverse_roots = jnp.where(renewal[:, None, None, None], renewed[None], old_roots)
    lefts, rights, slot_update = jax.vmap(slot_work)(pieces, stats_left, stats_right, inverse_roots)
    new_left = jnp.where(occupied[:, None, None], lefts, stats_left)
    new_right = jnp.where(occupied[:, None, None], rights, stats_right)
    placed = jnp.where(row_pick, slot_update[:, None], jnp.zeros((), jnp.bfloat16))
    outgoing = placed.reshape(capacity, fsdp_count, grp_count, row_count, block_size)
    returned = lax.all_to_all(
        lax.all_to_all(outgoing, "fsdp", split_axis=1, concat_axis=1, tiled=True),
        "grp",
        split_axis=2,
        concat_axis=2,
        tiled=True,
    )
    returned = returned.reshape(capacity * device_total, row_count, block_size)
    matrix_ids = jnp.arange(matrices, dtype=jnp.int32)[:, None]
    column_ids = jnp.arange(block_cols, dtype=jnp.int32)[None, :]
    wanted = ((matrix_ids * row_blocks + my_row) * block_cols + column_ids).reshape(-1)
    wanted_owner = owner[wanted]
    position = wanted_owner % capacity * device_total + wanted_owner // capacity
    gathered = returned[position].reshape(matrices, block_cols, row_count, block_size)
    update = gathered.transpose(0, 2, 1, 3).reshape(matrices, row_count, width)
    return (new_left, new_right, update)


def make_roles(owner, refresh, fsdp_count, grp_count, capacity, block_cols):
    plane_size = fsdp_count * ROLES
    blocks = jnp.arange(owner.shape[0], dtype=jnp.int32)
    device, slot = owner // capacity, owner % capacity
    column, plane = device // grp_count, device % grp_count
    renewed = refresh == 1
    root_plane = (plane + grp_count - 1) % grp_count
    own_role = plane * plane_size + column * ROLES + slot
    root_role = root_plane * plane_size + column * ROLES + capacity
    out_plane = jnp.where(renewed, root_plane, plane)
    order = blocks % block_cols * (owner.shape[0] // block_cols) + blocks // block_cols
    rows = (
        own_role,
        jnp.where(renewed, root_role, -1),
        jnp.where(renewed, root_role, own_role),
        plane * plane_size,
        root_plane * plane_size,
        out_plane * plane_size,
        plane * IN_CAP,
        root_plane * IN_CAP,
        out_plane * OUT_CAP,
        order,
    )
    roles = jnp.stack(rows)
    planes = jnp.arange(grp_count, dtype=jnp.int32)[:, None]
    owned = (plane[None, :] == planes).astype(jnp.int32)
    moved = ((root_plane[None, :] == planes) & renewed[None, :]).astype(jnp.int32)
    left_over = ((plane[None, :] == planes) & ~renewed[None, :]).astype(jnp.int32)
    over = jnp.maximum(jnp.sum(owned + moved, axis=1) - IN_CAP, jnp.sum(left_over + moved, axis=1) - OUT_CAP)
    return jnp.max(over) <= 0, roles


def fill_table(roles, table, my_grp, grp_count, plane_size):
    count = roles.shape[1]
    i32 = jnp.int32

    def spot(shape, axis):
        return lax.broadcasted_iota(i32, shape, axis)

    diagonal = spot((count, count), 0) == spot((count, count), 1)

    def upright(row):
        return jnp.sum(jnp.where(diagonal, roles[row : row + 1], 0), axis=1, keepdims=True)

    own, root, out, own_start, root_start, out_start, own_base, root_base, out_base, order = map(
        upright, range(10)
    )
    own_row, root_row, out_row = roles[0:1], roles[1:2], roles[2:3]

    def ahead(row, start, role):
        return jnp.sum(((row >= start) & (row < role)).astype(i32), axis=1, keepdims=True)

    own_at = ahead(own_row, own_start, own) + ahead(root_row, own_start, own)
    root_at = ahead(own_row, root_start, root) + ahead(root_row, root_start, root)
    out_at = ahead(out_row, out_start, out)

    def pick(key, wanted, value):
        return jnp.sum(jnp.where(key == wanted, value, 0), axis=0, keepdims=True)

    length = grp_count * IN_CAP
    entry = spot((count, length), 1)
    root_entry = jnp.where(root >= 0, root_base + root_at, -1)
    table[0:1, 0:length] = pick(own_base + own_at, entry, order) + pick(root_entry, entry, order)
    mine = my_grp * plane_size + spot((count, plane_size), 1)
    table[1:2, 0:plane_size] = pick(own, mine, own_at) + pick(root, mine, root_at)
    place = out_base + out_at
    table[2:3, 0:count] = jnp.sum(jnp.where(diagonal, place, 0), axis=0, keepdims=True)
    my_entry = my_grp * OUT_CAP + spot((count, OUT_CAP), 1)
    table[3:4, 0:OUT_CAP] = pick(place, my_entry, out - out_start)


def step_kernel(
    sizes,
    roles,
    grad_hbm,
    left_hbm,
    right_hbm,
    old_hbm,
    fresh_hbm,
    new_left_hbm,
    new_right_hbm,
    update,
    grad,
    out1,
    in1,
    out2,
    pieces,
    product,
    shaped,
    in3,
    out4,
    in4,
    roots,
    left,
    right,
    table,
    lookup,
    local_sem,
    self_sem,
    send_sem,
    recv_sem,
):
    fsdp_count, grp_count, capacity, rows, block, block_cols, matrices = sizes
    plane_rows = grp_count * rows
    width = block // CHUNKS
    f, g = lax.axis_index("fsdp"), lax.axis_index("grp")

    def along(k):
        return lax.rem(g + k, grp_count)

    def across(k):
        return lax.rem(f + k, fsdp_count)

    loads = [
        pltpu.make_async_copy(
            grad_hbm.at[:, :, pl.ds(j * block, block)],
            grad.at[pl.ds(j * matrices, matrices)],
            local_sem.at[0],
        )
        for j in range(block_cols)
    ] + [
        pltpu.make_async_copy(old_hbm, roots.at[pl.ds(0, capacity)], local_sem.at[1]),
        pltpu.make_async_copy(fresh_hbm, roots.at[pl.ds(capacity, 1)], local_sem.at[2]),
        pltpu.make_async_copy(left_hbm, left, local_sem.at[3]),
        pltpu.make_async_copy(right_hbm, right, local_sem.at[4]),
    ]
    for load in loads:
        load.start()

    barrier = pltpu.get_barrier_semaphore()

    @pl.loop(1, grp_count)
    def _(k):
        pl.semaphore_signal(barrier, 1, device_id=(f, along(k)), device_id_type=MESH)

    @pl.loop(1, fsdp_count)
    def _(k):
        pl.semaphore_signal(barrier, 1, device_id=(across(k), g), device_id_type=MESH)

    fill_table(roles, table, g, grp_count, fsdp_count * ROLES)
    to_scalars = pltpu.make_async_copy(table, lookup, local_sem.at[5])
    to_scalars.start()
    pltpu.make_async_copy(grad, grad, local_sem.at[0]).wait()
    to_scalars.wait()

    def gather_rows(chunks):
        @pl.loop(0, grp_count)
        def _(to):
            @pl.loop(0, IN_CAP, unroll=8)
            def _(i):
                both = grad[lookup[0, to * IN_CAP + i]]
                for c in chunks:
                    out1[c, to, i] = both[:, c * width : (c + 1) * width]

    def grp_copy(c, source, target, k, length, phase):
        return pltpu.make_async_remote_copy(
            src_ref=source.at[c, along(k)],
            dst_ref=target[c].at[pl.ds(g * length, length)],
            send_sem=send_sem.at[phase, c],
            recv_sem=recv_sem.at[phase, c],
            device_id=(f, along(k)),
            device_id_type=MESH,
        )

    def grp_wait(c, source, target, length, phase):
        everything = pltpu.make_async_remote_copy(
            src_ref=source.at[c, pl.ds(0, grp_count - 1)],
            dst_ref=target[c].at[pl.ds(0, (grp_count - 1) * length)],
            send_sem=send_sem.at[phase, c],
            recv_sem=recv_sem.at[phase, c],
            device_id=(f, g),
            device_id_type=MESH,
        )
        everything.wait_send()
        everything.wait_recv()

    def send_rows(c):
        pltpu.make_async_copy(out1.at[c, g], in1[c].at[pl.ds(g * IN_CAP, IN_CAP)], self_sem.at[0, c]).start()

        @pl.loop(1, grp_count)
        def _(k):
            grp_copy(c, out1, in1, k, IN_CAP, 0).start()

    gather_rows([0])
    pl.semaphore_wait(barrier, grp_count - 1 + fsdp_count - 1)
    send_rows(0)

    gather_rows(range(1, CHUNKS))
    for c in range(1, CHUNKS):
        send_rows(c)

    def spread(c):
        pltpu.make_async_copy(out1.at[c, g], in1[c].at[pl.ds(g * IN_CAP, IN_CAP)], self_sem.at[0, c]).wait()
        grp_wait(c, out1, in1, IN_CAP, 0)
        lanes = pl.ds(c * width, width)

        @pl.loop(0, fsdp_count)
        def _(k):
            to = across(k)
            for role in range(ROLES):
                i = lookup[1, to * ROLES + role]
                parts = [in1[c][source * IN_CAP + i] for source in range(grp_count)]
                out2[c, to * ROLES + role] = jnp.concatenate(parts, axis=0)

            source = out2.at[c, pl.ds(to * ROLES, ROLES)]
            target = pieces.at[:, pl.ds(pl.multiple_of(f * plane_rows, 16), plane_rows), lanes]

            @pl.when(k == 0)
            def _():
                pltpu.make_async_copy(source, target, self_sem.at[1, c]).start()

            @pl.when(k > 0)
            def _():
                pltpu.make_async_remote_copy(
                    src_ref=source,
                    dst_ref=target,
                    send_sem=send_sem.at[1, c],
                    recv_sem=recv_sem.at[1, c],
                    device_id=(to, g),
                    device_id_type=MESH,
                ).start()

    for c in range(CHUNKS):
        spread(c)

    def plane_wait(c, buffer, phase):
        everything = pltpu.make_async_remote_copy(
            src_ref=buffer.at[pl.ds(0, (fsdp_count - 1) * ROLES)],
            dst_ref=buffer.at[pl.ds(0, (fsdp_count - 1) * ROLES)],
            send_sem=send_sem.at[phase, c],
            recv_sem=recv_sem.at[phase, c],
            device_id=(f, g),
            device_id_type=MESH,
        )
        everything.wait_send()
        everything.wait_recv()

    def apply_left(h):
        lanes = pl.ds(h * (block // 2), block // 2)

        @pl.loop(0, ROLES)
        def _(role):
            piece = pieces[role, :, lanes]
            applied = jnp.dot(roots[role, 0], piece, preferred_element_type=jnp.float32).astype(jnp.bfloat16)
            share = jnp.dot(applied, roots[role, 1, lanes, :], preferred_element_type=jnp.float32)
            if h == 0:
                product[role] = share
            else:
                total = product[role] + share
                wide = pieces[role].astype(jnp.float32)
                count = 1.0 / (block * block)
                scale = jnp.sqrt(jnp.sum(wide * wide, keepdims=True) * count + epsilon) * lax.rsqrt(
                    jnp.sum(total * total, keepdims=True) * count + epsilon
                )
                shaped[role] = (total * scale).astype(jnp.bfloat16)

    loads[-4].wait()
    loads[-3].wait()
    for c in range(CHUNKS):
        own = out2.at[c, pl.ds(0, ROLES)]
        pltpu.make_async_copy(own, own, self_sem.at[1, c]).wait()
        plane_wait(c, out2.at[c], 1)
        if c == CHUNKS // 2 - 1:
            apply_left(0)
    apply_left(1)

    def send_back(c):
        lanes = pl.ds(c * width, width)

        @pl.loop(0, fsdp_count)
        def _(k):
            to = across(k)
            source = shaped.at[:, pl.ds(pl.multiple_of(to * plane_rows, 16), plane_rows), lanes]
            target = in3[c].at[pl.ds(f * ROLES, ROLES)]

            @pl.when(k == 0)
            def _():
                pltpu.make_async_copy(source, target, self_sem.at[2, c]).start()

            @pl.when(k > 0)
            def _():
                pltpu.make_async_remote_copy(
                    src_ref=source,
                    dst_ref=target,
                    send_sem=send_sem.at[2, c],
                    recv_sem=recv_sem.at[2, c],
                    device_id=(to, g),
                    device_id_type=MESH,
                ).start()

    def return_rows(c):
        own = in3[c].at[pl.ds(0, ROLES)]
        pltpu.make_async_copy(own, own, self_sem.at[2, c]).wait()
        plane_wait(c, in3[c], 2)

        @pl.loop(0, OUT_CAP, unroll=2)
        def _(i):
            tile = in3[c][lookup[3, i]]
            for to in range(grp_count):
                out4[c, to, i] = tile[to * rows : (to + 1) * rows]

        pltpu.make_async_copy(out4.at[c, g], in4[c].at[pl.ds(g * OUT_CAP, OUT_CAP)], self_sem.at[3, c]).start()

        @pl.loop(1, grp_count)
        def _(k):
            grp_copy(c, out4, in4, k, OUT_CAP, 3).start()

    def update_statistics(slot):
        piece = pieces[slot]
        held = jnp.sum((roles[0:1] == (g * fsdp_count + f) * ROLES + slot).astype(jnp.int32), axis=1, keepdims=True) > 0
        keep = jnp.where(held, jnp.float32(decay_rate), jnp.float32(1.0))
        add = jnp.where(held, jnp.float32(1.0 - decay_rate), jnp.float32(0.0))
        outer = lax.dot_general(piece, piece, (((1,), (1,)), ((), ())), preferred_element_type=jnp.float32)
        left[slot] = keep * left[slot] + add * outer
        inner = lax.dot_general(piece, piece, (((0,), (0,)), ((), ())), preferred_element_type=jnp.float32)
        right[slot] = keep * right[slot] + add * inner

    send_back(0)
    send_back(1)
    for c in range(2, CHUNKS):
        return_rows(c - 2)
        send_back(c)
    loads[-2].wait()
    loads[-1].wait()
    pl.loop(0, 1)(update_statistics)
    return_rows(CHUNKS - 2)
    return_rows(CHUNKS - 1)
    pl.loop(1, capacity)(update_statistics)
    stores = [
        pltpu.make_async_copy(left, new_left_hbm, local_sem.at[5]),
        pltpu.make_async_copy(right, new_right_hbm, local_sem.at[6]),
    ]
    for store in stores:
        store.start()
    for c in range(CHUNKS):
        pltpu.make_async_copy(out4.at[c, g], in4[c].at[pl.ds(g * OUT_CAP, OUT_CAP)], self_sem.at[3, c]).wait()
        grp_wait(c, out4, in4, OUT_CAP, 3)

        @pl.loop(0, matrices)
        def _(m):
            for j in range(block_cols):
                column = j * block + c * width
                update[m, :, pl.ds(column, width)] = in4[c][lookup[2, m * block_cols + j]]

    for store in stores:
        store.wait()


def listed_plan(roles, grad, stats_left, stats_right, old_roots, fresh_roots):
    matrices, rows, total_width = grad.shape
    capacity, block = stats_left.shape[0], stats_left.shape[1]
    fsdp_count, grp_count = lax.axis_size("fsdp"), lax.axis_size("grp")
    sizes = (fsdp_count, grp_count, capacity, rows, block, total_width // block, matrices)
    width, plane_rows = block // CHUNKS, grp_count * rows
    bf16 = jnp.bfloat16
    vmem, hbm = pl.BlockSpec(memory_space=pltpu.VMEM), pl.BlockSpec(memory_space=pl.ANY)
    return pl.pallas_call(
        functools.partial(step_kernel, sizes),
        out_shape=(
            jax.ShapeDtypeStruct(stats_left.shape, jnp.float32),
            jax.ShapeDtypeStruct(stats_right.shape, jnp.float32),
            jax.ShapeDtypeStruct(grad.shape, bf16),
        ),
        in_specs=[vmem] + [hbm] * 5,
        out_specs=(hbm, hbm, vmem),
        scratch_shapes=[
            pltpu.VMEM((matrices * (total_width // block), rows, block), bf16),
            pltpu.VMEM((CHUNKS, grp_count, IN_CAP, rows, width), bf16),
            [pltpu.VMEM((grp_count * IN_CAP, rows, width), bf16)] * CHUNKS,
            pltpu.VMEM((CHUNKS, fsdp_count * ROLES, plane_rows, width), bf16),
            pltpu.VMEM((ROLES, block, block), bf16),
            pltpu.VMEM((ROLES, block, block), jnp.float32),
            pltpu.VMEM((ROLES, block, block), bf16),
            [pltpu.VMEM((fsdp_count * ROLES, plane_rows, width), bf16)] * CHUNKS,
            pltpu.VMEM((CHUNKS, grp_count, OUT_CAP, rows, width), bf16),
            [pltpu.VMEM((grp_count * OUT_CAP, rows, width), bf16)] * CHUNKS,
            pltpu.VMEM((ROLES, 2, block, block), bf16),
            pltpu.VMEM(stats_left.shape, jnp.float32),
            pltpu.VMEM(stats_right.shape, jnp.float32),
            pltpu.VMEM((8, 512), jnp.int32),
            pltpu.SMEM((8, 512), jnp.int32),
            pltpu.SemaphoreType.DMA((7,)),
            pltpu.SemaphoreType.DMA((4, CHUNKS)),
            pltpu.SemaphoreType.DMA((4, CHUNKS)),
            pltpu.SemaphoreType.DMA((4, CHUNKS)),
        ],
        compiler_params=pltpu.CompilerParams(
            collective_id=1, has_side_effects=True, vmem_limit_bytes=28 * 1024 * 1024
        ),
        name="listed_step",
    )(roles, grad, stats_left, stats_right, old_roots, fresh_roots)


def local(grad, owner, refresh, stats_left, stats_right, old_roots, fresh_roots):
    fits, roles = make_roles(
        owner,
        refresh,
        lax.axis_size("fsdp"),
        lax.axis_size("grp"),
        stats_left.shape[0],
        grad.shape[2] // stats_left.shape[1],
    )
    return lax.cond(
        fits,
        lambda: listed_plan(roles, grad, stats_left, stats_right, old_roots, fresh_roots),
        lambda: dense_plan(grad, owner, refresh, stats_left, stats_right, old_roots, fresh_roots),
    )


def solution(mesh):
    return jax.shard_map(
        local,
        mesh=mesh,
        in_specs=(
            P(None, ("fsdp", "grp"), None),
            P(),
            P(),
            P(("fsdp", "grp"), None, None),
            P(("fsdp", "grp"), None, None),
            P(("fsdp", "grp"), None, None, None),
            P(("fsdp", "grp"), None, None, None),
        ),
        out_specs=(
            P(("fsdp", "grp"), None, None),
            P(("fsdp", "grp"), None, None),
            P(None, ("fsdp", "grp"), None),
        ),
        check_vma=False,
    )
```

```python
import functools

import jax
import jax.numpy as jnp
import numpy as np
from jax import lax
from jax.experimental import pallas as pl
from jax.experimental.pallas import tpu as pltpu
from jax.sharding import PartitionSpec as P

decay_rate = 0.999
epsilon = 1e-06

CHUNKS = 4
LISTS = ((48, 38), (64, 56))

MESH = pl.DeviceIdType.MESH


def shifted(block, axis, distance):
    devices = range(lax.axis_size(axis))
    route = [((i - distance) % len(devices), i) for i in devices]
    return lax.ppermute(block, axis, route)


def slot_work(piece, left, right, inverse_roots):
    new_left = decay_rate * left + (1.0 - decay_rate) * jnp.dot(
        piece, piece.T, preferred_element_type=jnp.float32
    )
    new_right = decay_rate * right + (1.0 - decay_rate) * jnp.dot(
        piece.T, piece, preferred_element_type=jnp.float32
    )
    left_applied = jnp.dot(inverse_roots[0], piece, preferred_element_type=jnp.float32).astype(
        jnp.bfloat16
    )
    shaped = jnp.dot(left_applied, inverse_roots[1], preferred_element_type=jnp.float32)
    wide = piece.astype(jnp.float32)
    graft_scale = jnp.sqrt(jnp.mean(wide * wide) + epsilon) / jnp.sqrt(
        jnp.mean(shaped * shaped) + epsilon
    )
    return (new_left, new_right, (shaped * graft_scale).astype(jnp.bfloat16))


def dense_plan(grad, owner, refresh, stats_left, stats_right, old_roots, fresh_roots):
    matrices, row_count, width = grad.shape
    capacity, block_size = (stats_left.shape[0], stats_left.shape[1])
    block_cols = width // block_size
    fsdp_count = lax.axis_size("fsdp")
    grp_count = lax.axis_size("grp")
    device_total = fsdp_count * grp_count
    row_blocks = row_count * device_total // block_size
    block_total = matrices * row_blocks * block_cols
    self_index = lax.axis_index("fsdp") * grp_count + lax.axis_index("grp")
    my_row = self_index // (device_total // row_blocks)
    local_blocks = grad.reshape(matrices, row_count, block_cols, block_size).transpose(0, 2, 1, 3)
    local_blocks = local_blocks.reshape(matrices * block_cols, row_count, block_size)
    slot_ids = jnp.arange(capacity, dtype=jnp.int32)[:, None, None]
    fsdp_ids = jnp.arange(fsdp_count, dtype=jnp.int32)[None, :, None]
    grp_ids = jnp.arange(grp_count, dtype=jnp.int32)[None, None, :]
    slot_order = ((fsdp_ids * grp_count + grp_ids) * capacity + slot_ids).reshape(-1)
    block_ids = jnp.arange(block_total, dtype=jnp.int32)
    matches = owner[None, :] == slot_order[:, None]
    present = jnp.any(matches, axis=1)
    chosen_block = jnp.sum(jnp.where(matches, block_ids[None, :], 0), axis=1)
    chosen_row = chosen_block // block_cols % row_blocks
    local_index = chosen_block // (row_blocks * block_cols) * block_cols + chosen_block % block_cols
    sending = present & (chosen_row == my_row)
    outbound = jnp.where(
        sending[:, None, None], local_blocks[local_index], jnp.zeros((), jnp.bfloat16)
    )
    outbound = outbound.reshape(capacity, fsdp_count, grp_count, row_count, block_size)
    inbound = lax.all_to_all(
        lax.all_to_all(outbound, "fsdp", split_axis=1, concat_axis=1, tiled=True),
        "grp",
        split_axis=2,
        concat_axis=2,
        tiled=True,
    )
    own_slots = self_index * capacity + jnp.arange(capacity, dtype=jnp.int32)
    own_matches = owner[None, :] == own_slots[:, None]
    occupied = jnp.any(own_matches, axis=1)
    own_block = jnp.sum(jnp.where(own_matches, block_ids[None, :], 0), axis=1)
    own_row = own_block // block_cols % row_blocks
    row_pick = (jnp.arange(row_blocks, dtype=jnp.int32)[None, :] == own_row[:, None])[
        :, :, None, None
    ]
    stacked = inbound.reshape(capacity, row_blocks, block_size, block_size)
    pieces = jnp.sum(jnp.where(row_pick, stacked, jnp.zeros((), jnp.bfloat16)), axis=1)
    renewal = jnp.sum(jnp.where(own_matches, refresh[None, :], 0), axis=1) == 1
    renewed = shifted(fresh_roots, "grp", 1)[0]
    inverse_roots = jnp.where(renewal[:, None, None, None], renewed[None], old_roots)
    lefts, rights, slot_update = jax.vmap(slot_work)(pieces, stats_left, stats_right, inverse_roots)
    new_left = jnp.where(occupied[:, None, None], lefts, stats_left)
    new_right = jnp.where(occupied[:, None, None], rights, stats_right)
    placed = jnp.where(row_pick, slot_update[:, None], jnp.zeros((), jnp.bfloat16))
    outgoing = placed.reshape(capacity, fsdp_count, grp_count, row_count, block_size)
    returned = lax.all_to_all(
        lax.all_to_all(outgoing, "fsdp", split_axis=1, concat_axis=1, tiled=True),
        "grp",
        split_axis=2,
        concat_axis=2,
        tiled=True,
    )
    returned = returned.reshape(capacity * device_total, row_count, block_size)
    matrix_ids = jnp.arange(matrices, dtype=jnp.int32)[:, None]
    column_ids = jnp.arange(block_cols, dtype=jnp.int32)[None, :]
    wanted = ((matrix_ids * row_blocks + my_row) * block_cols + column_ids).reshape(-1)
    wanted_owner = owner[wanted]
    position = wanted_owner % capacity * device_total + wanted_owner // capacity
    gathered = returned[position].reshape(matrices, block_cols, row_count, block_size)
    update = gathered.transpose(0, 2, 1, 3).reshape(matrices, row_count, width)
    return (new_left, new_right, update)


def halves(value, size):
    if size & (size - 1):
        return value // size, value % size
    return value >> (size.bit_length() - 1), value & (size - 1)


def too_short(owner, refresh, grp_count, capacity):
    plane = halves(halves(owner, capacity)[0], grp_count)[1]
    planes = np.arange(grp_count, dtype=np.int32)
    here = plane[None, :] == planes[:, None]
    there = plane[None, :] == np.roll(planes, -1)[:, None]
    owned = here.astype(jnp.int32)
    due = jnp.sum(owned + jnp.where(there, refresh[None, :], 0), axis=1)
    kept = jnp.sum(owned, axis=1)
    over = [jnp.max(jnp.maximum(due - here, kept - back)) > 0 for here, back in LISTS]
    return sum(each.astype(jnp.int32) for each in over)


def fill_table(owner_row, refresh_row, table, my_grp, fsdp_count, grp_count, capacity, block_cols, lengths):
    count, roles = owner_row.shape[1], capacity + 1
    in_length, out_length = lengths
    i32 = jnp.int32

    def spot(shape, axis):
        return lax.broadcasted_iota(i32, shape, axis)

    diagonal = spot((count, count), 0) == spot((count, count), 1)

    def upright(row):
        return jnp.sum(jnp.where(diagonal, row, 0), axis=1, keepdims=True)

    def views(owner, renewed):
        device, slot = halves(owner, capacity)
        column, plane = halves(device, grp_count)
        root_plane = jnp.where(plane == 0, grp_count - 1, plane - 1)
        own = (plane * fsdp_count + column) * roles + slot
        root = jnp.where(renewed, (root_plane * fsdp_count + column) * roles + capacity, -1)
        return plane, root_plane, column * capacity + slot, own, root

    _, _, _, own_row, root_row = views(owner_row, refresh_row == 1)
    renewed = upright(refresh_row) == 1
    plane, root_plane, home, own, root = views(upright(owner_row), renewed)
    own_start, root_start = plane * (fsdp_count * roles), root_plane * (fsdp_count * roles)

    def ahead(row, start, role):
        return jnp.sum(((row >= start) & (row < role)).astype(i32), axis=1, keepdims=True)

    out_at = ahead(own_row, own_start, own)
    own_at = out_at + ahead(root_row, own_start, own)
    root_at = ahead(own_row, root_start, root) + ahead(root_row, root_start, root)

    def pick(key, base, length, value):
        wanted = base + spot((count, length), 1)
        return jnp.sum(jnp.where(key == wanted, value, 0), axis=0, keepdims=True)

    block = spot((count, 1), 0)
    matrix = sum((block >= block_cols * m).astype(i32) for m in range(1, count // block_cols))
    order = (block - matrix * block_cols) * (count // block_cols) + matrix
    root_entry = jnp.where(renewed, root_plane * in_length + root_at, -1)
    length, plane_size = grp_count * in_length, fsdp_count * roles

    def put(row, values, limit):
        table[row : row + 1, 0 : values.shape[1]] = jnp.clip(values, 0, limit - 1)

    put(0, pick(plane * in_length + own_at, 0, length, order) + pick(root_entry, 0, length, order), count)
    put(1, pick(own, my_grp * plane_size, plane_size, own_at) + pick(root, my_grp * plane_size, plane_size, root_at), in_length)
    place = plane * out_length + out_at
    put(2, jnp.sum(jnp.where(diagonal, place, 0), axis=0, keepdims=True), grp_count * out_length)
    put(3, pick(place, my_grp * out_length, out_length, home), fsdp_count * capacity)


def both_ways(count):
    return [k for near in range(count // 2, 0, -1) for k in dict.fromkeys((near, count - near))]


def step_kernel(
    sizes,
    lengths,
    owner_row,
    refresh_row,
    grad_hbm,
    left_hbm,
    right_hbm,
    old_hbm,
    fresh_hbm,
    new_left_hbm,
    new_right_hbm,
    update,
    grad,
    out1,
    in1,
    out2,
    pieces,
    product,
    shaped,
    back,
    settled,
    in3,
    out4,
    in4,
    roots,
    left,
    right,
    table,
    lookup,
    local_sem,
    self_sem,
    send_sem,
    recv_sem,
):
    fsdp_count, grp_count, capacity, rows, block, block_cols, matrices = sizes
    plane_rows = grp_count * rows
    width = block // CHUNKS
    f, g = lax.axis_index("fsdp"), lax.axis_index("grp")
    roles_in = capacity + 1
    in_length, out_length = lengths

    def along(k):
        return lax.rem(g + k, grp_count)

    def across(k):
        return lax.rem(f + k, fsdp_count)

    loads = [
        pltpu.make_async_copy(
            grad_hbm.at[:, :, pl.ds(j * block, block)],
            grad.at[pl.ds(j * matrices, matrices)],
            local_sem.at[0],
        )
        for j in range(block_cols)
    ] + [
        pltpu.make_async_copy(old_hbm, roots.at[pl.ds(0, capacity)], local_sem.at[1]),
        pltpu.make_async_copy(fresh_hbm, roots.at[pl.ds(capacity, 1)], local_sem.at[2]),
        pltpu.make_async_copy(left_hbm, left, local_sem.at[3]),
        pltpu.make_async_copy(right_hbm, right, local_sem.at[4]),
    ]
    for load in loads:
        load.start()

    barrier = pltpu.get_barrier_semaphore()

    @pl.loop(1, grp_count)
    def _(k):
        pl.semaphore_signal(barrier, 1, device_id=(f, along(k)), device_id_type=MESH)

    @pl.loop(1, fsdp_count)
    def _(k):
        pl.semaphore_signal(barrier, 1, device_id=(across(k), g), device_id_type=MESH)

    fill_table(
        owner_row[...], refresh_row[...], table, g, fsdp_count, grp_count, capacity, block_cols, lengths
    )
    to_scalars = pltpu.make_async_copy(table, lookup, local_sem.at[5])
    to_scalars.start()
    pltpu.make_async_copy(grad, grad, local_sem.at[0]).wait()
    to_scalars.wait()

    def remote(source, target, phase, c, device):
        return pltpu.make_async_remote_copy(
            src_ref=source,
            dst_ref=target,
            send_sem=send_sem.at[phase, c],
            recv_sem=recv_sem.at[phase, c],
            device_id=device,
            device_id_type=MESH,
        )

    def stays(source, target, phase, c):
        return pltpu.make_async_copy(source, target, self_sem.at[phase, c])

    def finish(source, target, phase, c):
        everything = remote(source, target, phase, c, (f, g))
        everything.wait_send()
        everything.wait_recv()

    def send_lists(source, target, length, phase, c):
        spot = target.at[pl.ds(g * length, length)]
        for k in both_ways(grp_count):
            remote(source.at[c, along(k)], spot, phase, c, (f, along(k))).start()
        stays(source.at[c, g], spot, phase, c).start()

    def await_lists(source, target, length, phase, c):
        stays(source.at[c, 0], target.at[pl.ds(0, length)], phase, c).wait()
        others = grp_count - 1
        finish(source.at[c, pl.ds(0, others)], target.at[pl.ds(0, others * length)], phase, c)

    def send_bands(source_of, target, phase, c):
        def send(k):
            remote(source_of(across(k)), target, phase, c, (across(k), g)).start()

        send(fsdp_count // 2)

        @pl.loop(1, fsdp_count // 2)
        def _(k):
            send(k)
            send(fsdp_count - k)

        stays(source_of(f), target, phase, c).start()

    def await_bands(buffer, roles, phase, c):
        own = buffer.at[pl.ds(0, roles)]
        stays(own, own, phase, c).wait()
        others = buffer.at[pl.ds(0, (fsdp_count - 1) * roles)]
        finish(others, others, phase, c)

    def lanes(c):
        return pl.ds(c * width, width)

    def band(to):
        return pl.ds(pl.multiple_of(to * plane_rows, 16), plane_rows)

    def gather_rows(chunks):
        @pl.loop(0, grp_count)
        def _(to):
            @pl.loop(0, in_length, unroll=4)
            def _(i):
                both = grad[lookup[0, to * in_length + i]]
                for c in chunks:
                    out1[c, to, i] = both[:, c * width : (c + 1) * width]

    def spread_rows(c):
        await_lists(out1, in1[c], in_length, 0, c)

        def collect(to):
            for role in range(roles_in):
                i = lookup[1, to * roles_in + role]
                tiles = [in1[c][source * in_length + i] for source in range(grp_count)]
                out2[c, to * roles_in + role] = jnp.concatenate(tiles, axis=0)
            return out2.at[c, pl.ds(to * roles_in, roles_in)]

        send_bands(collect, pieces.at[:, band(f), lanes(c)], 1, c)

    def apply_roots(role, h):
        some = pl.ds(h * (block // 2), block // 2)
        applied = jnp.dot(roots[role, 0], pieces[role, :, some], preferred_element_type=jnp.float32)
        total = jnp.dot(applied.astype(jnp.bfloat16), roots[role, 1, some, :], preferred_element_type=jnp.float32)
        if h == 0:
            product[role] = total
        else:
            total = product[role] + total
            wide = pieces[role].astype(jnp.float32)
            count = 1.0 / (block * block)
            scale = jnp.sqrt(jnp.sum(wide * wide, keepdims=True) * count + epsilon) * lax.rsqrt(
                jnp.sum(total * total, keepdims=True) * count + epsilon
            )
            shaped[role] = (total * scale).astype(jnp.bfloat16)

    def hop(c, to):
        return remote(shaped.at[capacity, :, lanes(c)], back.at[c], 4, c, (f, to))

    def mine(slot):
        return owner_row[...] == (f * grp_count + g) * capacity + slot

    def send_back(c):
        hop(c, along(1)).wait_recv()
        for slot in range(capacity):
            renewed = jnp.sum(jnp.where(mine(slot), refresh_row[...], 0), axis=1, keepdims=True) == 1
            settled[slot, :, lanes(c)] = jnp.where(renewed, back[c], shaped[slot, :, lanes(c)])
        target = in3[c].at[pl.ds(f * capacity, capacity)]
        send_bands(lambda to: settled.at[:, band(to), lanes(c)], target, 2, c)

    def return_rows(c):
        await_bands(in3[c], capacity, 2, c)

        @pl.loop(0, out_length, unroll=2)
        def _(i):
            tile = in3[c][lookup[3, i]]
            for to in range(grp_count):
                out4[c, to, i] = tile[to * rows : (to + 1) * rows]

        send_lists(out4, in4[c], out_length, 3, c)

    def update_statistics(slot):
        piece = pieces[slot]
        held = jnp.sum(mine(slot).astype(jnp.int32), axis=1, keepdims=True) > 0
        keep = jnp.where(held, jnp.float32(decay_rate), jnp.float32(1.0))
        add = jnp.where(held, jnp.float32(1.0 - decay_rate), jnp.float32(0.0))
        outer = lax.dot_general(piece, piece, (((1,), (1,)), ((), ())), preferred_element_type=jnp.float32)
        left[slot] = keep * left[slot] + add * outer
        inner = lax.dot_general(piece, piece, (((0,), (0,)), ((), ())), preferred_element_type=jnp.float32)
        right[slot] = keep * right[slot] + add * inner

    gather_rows([0])
    pl.semaphore_wait(barrier, grp_count - 1 + fsdp_count - 1)
    send_lists(out1, in1[0], in_length, 0, 0)
    gather_rows(range(1, CHUNKS))
    for c in range(1, CHUNKS):
        send_lists(out1, in1[c], in_length, 0, c)

    for c in range(CHUNKS):
        spread_rows(c)
    loads[-4].wait()
    loads[-3].wait()
    for c in range(CHUNKS):
        await_bands(out2.at[c], roles_in, 1, c)
        if c == CHUNKS // 2 - 1:
            pl.loop(0, roles_in)(lambda role: apply_roots(role, 0))
    pl.loop(capacity, roles_in)(lambda role: apply_roots(role, 1))
    for c in range(CHUNKS):
        hop(c, along(1)).start()
    pl.loop(0, capacity)(lambda role: apply_roots(role, 1))
    send_back(0)
    send_back(1)
    for c in range(2, CHUNKS):
        return_rows(c - 2)
        send_back(c)
    loads[-2].wait()
    loads[-1].wait()
    pl.loop(0, 1)(update_statistics)
    return_rows(CHUNKS - 2)
    return_rows(CHUNKS - 1)
    pl.loop(1, capacity)(update_statistics)
    stores = [
        pltpu.make_async_copy(left, new_left_hbm, local_sem.at[5]),
        pltpu.make_async_copy(right, new_right_hbm, local_sem.at[6]),
    ]
    for store in stores:
        store.start()

    for c in range(CHUNKS):
        hop(c, along(1)).wait_send()
        await_lists(out4, in4[c], out_length, 3, c)

        @pl.loop(0, matrices)
        def _(m):
            for j in range(block_cols):
                column = j * block + c * width
                update[m, :, pl.ds(column, width)] = in4[c][lookup[2, m * block_cols + j]]

    for store in stores:
        store.wait()


def listed_plan(level, owner, refresh, grad, stats_left, stats_right, old_roots, fresh_roots):
    matrices, rows, total_width = grad.shape
    capacity, block = stats_left.shape[0], stats_left.shape[1]
    fsdp_count, grp_count = lax.axis_size("fsdp"), lax.axis_size("grp")
    sizes = (fsdp_count, grp_count, capacity, rows, block, total_width // block, matrices)
    width, plane_rows = block // CHUNKS, grp_count * rows
    bf16, f32 = jnp.bfloat16, jnp.float32
    roles = capacity + 1
    in_length, out_length = LISTS[level]
    vmem, hbm = pl.BlockSpec(memory_space=pltpu.VMEM), pl.BlockSpec(memory_space=pl.ANY)
    return pl.pallas_call(
        functools.partial(step_kernel, sizes, LISTS[level]),
        out_shape=(
            jax.ShapeDtypeStruct(stats_left.shape, f32),
            jax.ShapeDtypeStruct(stats_right.shape, f32),
            jax.ShapeDtypeStruct(grad.shape, bf16),
        ),
        in_specs=[vmem] * 2 + [hbm] * 5,
        out_specs=(hbm, hbm, vmem),
        scratch_shapes=[
            pltpu.VMEM((matrices * (total_width // block), rows, block), bf16),
            pltpu.VMEM((CHUNKS, grp_count, in_length, rows, width), bf16),
            [pltpu.VMEM((grp_count * in_length, rows, width), bf16)] * CHUNKS,
            pltpu.VMEM((CHUNKS, fsdp_count * roles, plane_rows, width), bf16),
            pltpu.VMEM((roles, block, block), bf16),
            pltpu.VMEM((roles, block, block), f32),
            pltpu.VMEM((roles, block, block), bf16),
            pltpu.VMEM((CHUNKS, block, width), bf16),
            pltpu.VMEM((capacity, block, block), bf16),
            [pltpu.VMEM((fsdp_count * capacity, plane_rows, width), bf16)] * CHUNKS,
            pltpu.VMEM((CHUNKS, grp_count, out_length, rows, width), bf16),
            [pltpu.VMEM((grp_count * out_length, rows, width), bf16)] * CHUNKS,
            pltpu.VMEM((roles, 2, block, block), bf16),
            pltpu.VMEM(stats_left.shape, f32),
            pltpu.VMEM(stats_right.shape, f32),
            pltpu.VMEM((8, 512), jnp.int32),
            pltpu.SMEM((8, 512), jnp.int32),
            pltpu.SemaphoreType.DMA((7,)),
            pltpu.SemaphoreType.DMA((4, CHUNKS)),
            pltpu.SemaphoreType.DMA((5, CHUNKS)),
            pltpu.SemaphoreType.DMA((5, CHUNKS)),
        ],
        compiler_params=pltpu.CompilerParams(
            collective_id=1 + level, has_side_effects=True, vmem_limit_bytes=28 * 1024 * 1024
        ),
        name="listed_step",
    )(owner[None], refresh[None], grad, stats_left, stats_right, old_roots, fresh_roots)


def hand_over_kernel(pieces, *refs):
    count = len(refs) // 3
    into, out_of = refs[-2:]
    moves = []
    for n in range(count):
        source, target, room = refs[n], refs[count + n], refs[2 * count + n]
        share = source.shape[0] // pieces
        for p in range(pieces):
            some, i = pl.ds(p * share, share), n * pieces + p
            moves.append(
                (
                    pltpu.make_async_copy(source.at[some], room.at[some], into.at[i]),
                    pltpu.make_async_copy(room.at[some], target.at[some], out_of.at[i]),
                )
            )
    for fetch, _ in moves:
        fetch.start()
    for fetch, store in moves:
        fetch.wait()
        store.start()
    for _, store in moves:
        store.wait()


def hand_over(*arrays):
    pieces = 2
    hbm = pl.BlockSpec(memory_space=pl.ANY)
    sems = pltpu.SemaphoreType.DMA((len(arrays) * pieces,))
    return pl.pallas_call(
        functools.partial(hand_over_kernel, pieces),
        out_shape=[jax.ShapeDtypeStruct(a.shape, a.dtype) for a in arrays],
        in_specs=[hbm] * len(arrays),
        out_specs=[hbm] * len(arrays),
        scratch_shapes=[pltpu.VMEM(a.shape, a.dtype) for a in arrays] + [sems, sems],
        compiler_params=pltpu.CompilerParams(vmem_limit_bytes=16 * 1024 * 1024),
        name="hand_over",
    )(*arrays)


def local(*arrays):
    grad, owner, refresh, *held = arrays
    branch = too_short(owner, refresh, lax.axis_size("grp"), held[0].shape[0])
    plans = [
        lambda level=level: listed_plan(level, owner, refresh, grad, *held) for level in range(len(LISTS))
    ]
    return tuple(hand_over(*lax.switch(branch, [*plans, lambda: dense_plan(*arrays)])))


def solution(mesh):
    return jax.shard_map(
        local,
        mesh=mesh,
        in_specs=(
            P(None, ("fsdp", "grp"), None),
            P(),
            P(),
            P(("fsdp", "grp"), None, None),
            P(("fsdp", "grp"), None, None),
            P(("fsdp", "grp"), None, None, None),
            P(("fsdp", "grp"), None, None, None),
        ),
        out_specs=(
            P(("fsdp", "grp"), None, None),
            P(("fsdp", "grp"), None, None),
            P(None, ("fsdp", "grp"), None),
        ),
        check_vma=False,
    )
```

```python
import functools

import jax
import jax.numpy as jnp
import numpy as np
from jax import lax
from jax.experimental import pallas as pl
from jax.experimental.pallas import tpu as pltpu
from jax.sharding import PartitionSpec as P

decay_rate = 0.999
epsilon = 1e-06

CHUNKS = 4
LISTS = ((48, 38), (54, 44))

MESH = pl.DeviceIdType.MESH


def shifted(block, axis, distance):
    devices = range(lax.axis_size(axis))
    route = [((i - distance) % len(devices), i) for i in devices]
    return lax.ppermute(block, axis, route)


def slot_work(piece, left, right, inverse_roots):
    new_left = decay_rate * left + (1.0 - decay_rate) * jnp.dot(
        piece, piece.T, preferred_element_type=jnp.float32
    )
    new_right = decay_rate * right + (1.0 - decay_rate) * jnp.dot(
        piece.T, piece, preferred_element_type=jnp.float32
    )
    left_applied = jnp.dot(inverse_roots[0], piece, preferred_element_type=jnp.float32).astype(
        jnp.bfloat16
    )
    shaped = jnp.dot(left_applied, inverse_roots[1], preferred_element_type=jnp.float32)
    wide = piece.astype(jnp.float32)
    graft_scale = jnp.sqrt(jnp.mean(wide * wide) + epsilon) / jnp.sqrt(
        jnp.mean(shaped * shaped) + epsilon
    )
    return (new_left, new_right, (shaped * graft_scale).astype(jnp.bfloat16))


def dense_plan(grad, owner, refresh, stats_left, stats_right, old_roots, fresh_roots):
    matrices, row_count, width = grad.shape
    capacity, block_size = (stats_left.shape[0], stats_left.shape[1])
    block_cols = width // block_size
    fsdp_count = lax.axis_size("fsdp")
    grp_count = lax.axis_size("grp")
    device_total = fsdp_count * grp_count
    row_blocks = row_count * device_total // block_size
    block_total = matrices * row_blocks * block_cols
    self_index = lax.axis_index("fsdp") * grp_count + lax.axis_index("grp")
    my_row = self_index // (device_total // row_blocks)
    local_blocks = grad.reshape(matrices, row_count, block_cols, block_size).transpose(0, 2, 1, 3)
    local_blocks = local_blocks.reshape(matrices * block_cols, row_count, block_size)
    slot_ids = jnp.arange(capacity, dtype=jnp.int32)[:, None, None]
    fsdp_ids = jnp.arange(fsdp_count, dtype=jnp.int32)[None, :, None]
    grp_ids = jnp.arange(grp_count, dtype=jnp.int32)[None, None, :]
    slot_order = ((fsdp_ids * grp_count + grp_ids) * capacity + slot_ids).reshape(-1)
    block_ids = jnp.arange(block_total, dtype=jnp.int32)
    matches = owner[None, :] == slot_order[:, None]
    present = jnp.any(matches, axis=1)
    chosen_block = jnp.sum(jnp.where(matches, block_ids[None, :], 0), axis=1)
    chosen_row = chosen_block // block_cols % row_blocks
    local_index = chosen_block // (row_blocks * block_cols) * block_cols + chosen_block % block_cols
    sending = present & (chosen_row == my_row)
    outbound = jnp.where(
        sending[:, None, None], local_blocks[local_index], jnp.zeros((), jnp.bfloat16)
    )
    outbound = outbound.reshape(capacity, fsdp_count, grp_count, row_count, block_size)
    inbound = lax.all_to_all(
        lax.all_to_all(outbound, "fsdp", split_axis=1, concat_axis=1, tiled=True),
        "grp",
        split_axis=2,
        concat_axis=2,
        tiled=True,
    )
    own_slots = self_index * capacity + jnp.arange(capacity, dtype=jnp.int32)
    own_matches = owner[None, :] == own_slots[:, None]
    occupied = jnp.any(own_matches, axis=1)
    own_block = jnp.sum(jnp.where(own_matches, block_ids[None, :], 0), axis=1)
    own_row = own_block // block_cols % row_blocks
    row_pick = (jnp.arange(row_blocks, dtype=jnp.int32)[None, :] == own_row[:, None])[
        :, :, None, None
    ]
    stacked = inbound.reshape(capacity, row_blocks, block_size, block_size)
    pieces = jnp.sum(jnp.where(row_pick, stacked, jnp.zeros((), jnp.bfloat16)), axis=1)
    renewal = jnp.sum(jnp.where(own_matches, refresh[None, :], 0), axis=1) == 1
    renewed = shifted(fresh_roots, "grp", 1)[0]
    inverse_roots = jnp.where(renewal[:, None, None, None], renewed[None], old_roots)
    lefts, rights, slot_update = jax.vmap(slot_work)(pieces, stats_left, stats_right, inverse_roots)
    new_left = jnp.where(occupied[:, None, None], lefts, stats_left)
    new_right = jnp.where(occupied[:, None, None], rights, stats_right)
    placed = jnp.where(row_pick, slot_update[:, None], jnp.zeros((), jnp.bfloat16))
    outgoing = placed.reshape(capacity, fsdp_count, grp_count, row_count, block_size)
    returned = lax.all_to_all(
        lax.all_to_all(outgoing, "fsdp", split_axis=1, concat_axis=1, tiled=True),
        "grp",
        split_axis=2,
        concat_axis=2,
        tiled=True,
    )
    returned = returned.reshape(capacity * device_total, row_count, block_size)
    matrix_ids = jnp.arange(matrices, dtype=jnp.int32)[:, None]
    column_ids = jnp.arange(block_cols, dtype=jnp.int32)[None, :]
    wanted = ((matrix_ids * row_blocks + my_row) * block_cols + column_ids).reshape(-1)
    wanted_owner = owner[wanted]
    position = wanted_owner % capacity * device_total + wanted_owner // capacity
    gathered = returned[position].reshape(matrices, block_cols, row_count, block_size)
    update = gathered.transpose(0, 2, 1, 3).reshape(matrices, row_count, width)
    return (new_left, new_right, update)


def halves(value, size):
    if size & (size - 1):
        return value // size, value % size
    return value >> (size.bit_length() - 1), value & (size - 1)


def too_short(owner, refresh, grp_count, capacity):
    plane = halves(halves(owner, capacity)[0], grp_count)[1]
    planes = np.arange(grp_count, dtype=np.int32)
    here = plane[None, :] == planes[:, None]
    there = plane[None, :] == np.roll(planes, -1)[:, None]
    owned = here.astype(jnp.int32)
    due = jnp.sum(owned + jnp.where(there, refresh[None, :], 0), axis=1)
    kept = jnp.sum(owned, axis=1)
    over = [jnp.max(jnp.maximum(due - here, kept - back)) > 0 for here, back in LISTS]
    return sum(each.astype(jnp.int32) for each in over)


def fill_table(owner_row, refresh_row, table, my_grp, fsdp_count, grp_count, capacity, block_cols, lengths):
    count, roles = owner_row.shape[1], capacity + 1
    in_length, out_length = lengths
    i32 = jnp.int32

    def spot(shape, axis):
        return lax.broadcasted_iota(i32, shape, axis)

    diagonal = spot((count, count), 0) == spot((count, count), 1)

    def upright(row):
        return jnp.sum(jnp.where(diagonal, row, 0), axis=1, keepdims=True)

    def views(owner, renewed):
        device, slot = halves(owner, capacity)
        column, plane = halves(device, grp_count)
        root_plane = jnp.where(plane == 0, grp_count - 1, plane - 1)
        own = (plane * fsdp_count + column) * roles + slot
        root = jnp.where(renewed, (root_plane * fsdp_count + column) * roles + capacity, -1)
        return plane, root_plane, column * capacity + slot, own, root

    _, _, _, own_row, root_row = views(owner_row, refresh_row == 1)
    renewed = upright(refresh_row) == 1
    plane, root_plane, home, own, root = views(upright(owner_row), renewed)
    own_start, root_start = plane * (fsdp_count * roles), root_plane * (fsdp_count * roles)

    def ahead(row, start, role):
        return jnp.sum(((row >= start) & (row < role)).astype(i32), axis=1, keepdims=True)

    out_at = ahead(own_row, own_start, own)
    own_at = out_at + ahead(root_row, own_start, own)
    root_at = ahead(own_row, root_start, root) + ahead(root_row, root_start, root)

    def pick(key, base, length, value):
        wanted = base + spot((count, length), 1)
        return jnp.sum(jnp.where(key == wanted, value, 0), axis=0, keepdims=True)

    block = spot((count, 1), 0)
    matrix = sum((block >= block_cols * m).astype(i32) for m in range(1, count // block_cols))
    order = (block - matrix * block_cols) * (count // block_cols) + matrix
    root_entry = jnp.where(renewed, root_plane * in_length + root_at, -1)
    length, plane_size = grp_count * in_length, fsdp_count * roles

    def put(row, values, limit):
        table[row : row + 1, 0 : values.shape[1]] = jnp.clip(values, 0, limit - 1)

    put(0, pick(plane * in_length + own_at, 0, length, order) + pick(root_entry, 0, length, order), count)
    put(1, pick(own, my_grp * plane_size, plane_size, own_at) + pick(root, my_grp * plane_size, plane_size, root_at), in_length)
    place = plane * out_length + out_at
    put(2, jnp.sum(jnp.where(diagonal, place, 0), axis=0, keepdims=True), grp_count * out_length)
    put(3, pick(place, my_grp * out_length, out_length, home), fsdp_count * capacity)


def both_ways(count):
    return [k for near in range(count // 2, 0, -1) for k in dict.fromkeys((near, count - near))]


def step_kernel(
    sizes,
    lengths,
    owner_row,
    refresh_row,
    grad_hbm,
    left_hbm,
    right_hbm,
    old_hbm,
    fresh_hbm,
    new_left_hbm,
    new_right_hbm,
    update,
    grad,
    out1,
    in1,
    out2,
    pieces,
    product,
    shaped,
    back,
    settled,
    in3,
    out4,
    in4,
    roots,
    left,
    right,
    table,
    lookup,
    local_sem,
    self_sem,
    send_sem,
    recv_sem,
):
    fsdp_count, grp_count, capacity, rows, block, block_cols, matrices = sizes
    plane_rows = grp_count * rows
    width = block // CHUNKS
    f, g = lax.axis_index("fsdp"), lax.axis_index("grp")
    roles_in = capacity + 1
    in_length, out_length = lengths

    def along(k):
        return lax.rem(g + k, grp_count)

    def across(k):
        return lax.rem(f + k, fsdp_count)

    loads = [
        pltpu.make_async_copy(
            grad_hbm.at[:, :, pl.ds(j * block, block)],
            grad.at[pl.ds(j * matrices, matrices)],
            local_sem.at[0],
        )
        for j in range(block_cols)
    ] + [
        pltpu.make_async_copy(old_hbm, roots.at[pl.ds(0, capacity)], local_sem.at[1]),
        pltpu.make_async_copy(fresh_hbm, roots.at[pl.ds(capacity, 1)], local_sem.at[2]),
        pltpu.make_async_copy(left_hbm, left, local_sem.at[3]),
        pltpu.make_async_copy(right_hbm, right, local_sem.at[4]),
    ]
    for load in loads:
        load.start()

    barrier = pltpu.get_barrier_semaphore()

    @pl.loop(1, grp_count)
    def _(k):
        pl.semaphore_signal(barrier, 1, device_id=(f, along(k)), device_id_type=MESH)

    @pl.loop(1, fsdp_count)
    def _(k):
        pl.semaphore_signal(barrier, 1, device_id=(across(k), g), device_id_type=MESH)

    fill_table(
        owner_row[...], refresh_row[...], table, g, fsdp_count, grp_count, capacity, block_cols, lengths
    )
    to_scalars = pltpu.make_async_copy(table, lookup, local_sem.at[5])
    to_scalars.start()
    pltpu.make_async_copy(grad, grad, local_sem.at[0]).wait()
    to_scalars.wait()

    def remote(source, target, phase, c, device):
        return pltpu.make_async_remote_copy(
            src_ref=source,
            dst_ref=target,
            send_sem=send_sem.at[phase, c],
            recv_sem=recv_sem.at[phase, c],
            device_id=device,
            device_id_type=MESH,
        )

    def stays(source, target, phase, c):
        return pltpu.make_async_copy(source, target, self_sem.at[phase, c])

    def finish(source, target, phase, c):
        everything = remote(source, target, phase, c, (f, g))
        everything.wait_send()
        everything.wait_recv()

    def send_lists(source, target, length, phase, c):
        spot = target.at[pl.ds(g * length, length)]
        for k in both_ways(grp_count):
            remote(source.at[c, along(k)], spot, phase, c, (f, along(k))).start()
        stays(source.at[c, g], spot, phase, c).start()

    def await_lists(source, target, length, phase, c):
        stays(source.at[c, 0], target.at[pl.ds(0, length)], phase, c).wait()
        others = grp_count - 1
        finish(source.at[c, pl.ds(0, others)], target.at[pl.ds(0, others * length)], phase, c)

    def send_bands(source_of, target, phase, c):
        def send(k):
            remote(source_of(across(k)), target, phase, c, (across(k), g)).start()

        send(fsdp_count // 2)

        @pl.loop(1, fsdp_count // 2)
        def _(k):
            send(k)
            send(fsdp_count - k)

        stays(source_of(f), target, phase, c).start()

    def await_bands(buffer, roles, phase, c):
        own = buffer.at[pl.ds(0, roles)]
        stays(own, own, phase, c).wait()
        others = buffer.at[pl.ds(0, (fsdp_count - 1) * roles)]
        finish(others, others, phase, c)

    def lanes(c):
        return pl.ds(c * width, width)

    def band(to):
        return pl.ds(pl.multiple_of(to * plane_rows, 16), plane_rows)

    def gather_rows(chunks):
        @pl.loop(0, grp_count)
        def _(to):
            @pl.loop(0, in_length, unroll=4)
            def _(i):
                both = grad[lookup[0, to * in_length + i]]
                for c in chunks:
                    out1[c, to, i] = both[:, c * width : (c + 1) * width]

    def spread_rows(c):
        await_lists(out1, in1[c], in_length, 0, c)

        def collect(to):
            for role in range(roles_in):
                i = lookup[1, to * roles_in + role]
                tiles = [in1[c][source * in_length + i] for source in range(grp_count)]
                out2[c, to * roles_in + role] = jnp.concatenate(tiles, axis=0)
            return out2.at[c, pl.ds(to * roles_in, roles_in)]

        send_bands(collect, pieces.at[:, band(f), lanes(c)], 1, c)

    def apply_roots(role, h):
        some = pl.ds(h * (block // 2), block // 2)
        applied = jnp.dot(roots[role, 0], pieces[role, :, some], preferred_element_type=jnp.float32)
        total = jnp.dot(applied.astype(jnp.bfloat16), roots[role, 1, some, :], preferred_element_type=jnp.float32)
        if h == 0:
            product[role] = total
        else:
            total = product[role] + total
            wide = pieces[role].astype(jnp.float32)
            count = 1.0 / (block * block)
            scale = jnp.sqrt(jnp.sum(wide * wide, keepdims=True) * count + epsilon) * lax.rsqrt(
                jnp.sum(total * total, keepdims=True) * count + epsilon
            )
            shaped[role] = (total * scale).astype(jnp.bfloat16)

    def hop(c, to):
        return remote(shaped.at[capacity, :, lanes(c)], back.at[c], 4, c, (f, to))

    def mine(slot):
        return owner_row[...] == (f * grp_count + g) * capacity + slot

    def send_back(c):
        hop(c, along(1)).wait_recv()
        for slot in range(capacity):
            renewed = jnp.sum(jnp.where(mine(slot), refresh_row[...], 0), axis=1, keepdims=True) == 1
            settled[slot, :, lanes(c)] = jnp.where(renewed, back[c], shaped[slot, :, lanes(c)])
        target = in3[c].at[pl.ds(f * capacity, capacity)]
        send_bands(lambda to: settled.at[:, band(to), lanes(c)], target, 2, c)

    def return_rows(c):
        await_bands(in3[c], capacity, 2, c)

        @pl.loop(0, out_length, unroll=2)
        def _(i):
            tile = in3[c][lookup[3, i]]
            for to in range(grp_count):
                out4[c, to, i] = tile[to * rows : (to + 1) * rows]

        send_lists(out4, in4[c], out_length, 3, c)

    def update_statistics(slot):
        piece = pieces[slot]
        held = jnp.sum(mine(slot).astype(jnp.int32), axis=1, keepdims=True) > 0
        keep = jnp.where(held, jnp.float32(decay_rate), jnp.float32(1.0))
        add = jnp.where(held, jnp.float32(1.0 - decay_rate), jnp.float32(0.0))
        outer = lax.dot_general(piece, piece, (((1,), (1,)), ((), ())), preferred_element_type=jnp.float32)
        left[slot] = keep * left[slot] + add * outer
        inner = lax.dot_general(piece, piece, (((0,), (0,)), ((), ())), preferred_element_type=jnp.float32)
        right[slot] = keep * right[slot] + add * inner

    gather_rows([0])
    pl.semaphore_wait(barrier, grp_count - 1 + fsdp_count - 1)
    send_lists(out1, in1[0], in_length, 0, 0)
    gather_rows(range(1, CHUNKS))
    for c in range(1, CHUNKS):
        send_lists(out1, in1[c], in_length, 0, c)

    for c in range(CHUNKS):
        spread_rows(c)
    loads[-4].wait()
    loads[-3].wait()
    for c in range(CHUNKS):
        await_bands(out2.at[c], roles_in, 1, c)
        if c == CHUNKS // 2 - 1:
            pl.loop(0, roles_in)(lambda role: apply_roots(role, 0))
    pl.loop(capacity, roles_in)(lambda role: apply_roots(role, 1))
    for c in range(CHUNKS):
        hop(c, along(1)).start()
    pl.loop(0, capacity)(lambda role: apply_roots(role, 1))
    send_back(0)
    send_back(1)
    for c in range(2, CHUNKS):
        return_rows(c - 2)
        send_back(c)
    loads[-2].wait()
    loads[-1].wait()
    pl.loop(0, 1)(update_statistics)
    return_rows(CHUNKS - 2)
    return_rows(CHUNKS - 1)
    pl.loop(1, capacity)(update_statistics)
    stores = [
        pltpu.make_async_copy(left, new_left_hbm, local_sem.at[5]),
        pltpu.make_async_copy(right, new_right_hbm, local_sem.at[6]),
    ]
    for store in stores:
        store.start()

    for c in range(CHUNKS):
        hop(c, along(1)).wait_send()
        await_lists(out4, in4[c], out_length, 3, c)

        @pl.loop(0, matrices)
        def _(m):
            for j in range(block_cols):
                column = j * block + c * width
                update[m, :, pl.ds(column, width)] = in4[c][lookup[2, m * block_cols + j]]

    for store in stores:
        store.wait()


def listed_plan(level, owner, refresh, grad, stats_left, stats_right, old_roots, fresh_roots):
    matrices, rows, total_width = grad.shape
    capacity, block = stats_left.shape[0], stats_left.shape[1]
    fsdp_count, grp_count = lax.axis_size("fsdp"), lax.axis_size("grp")
    sizes = (fsdp_count, grp_count, capacity, rows, block, total_width // block, matrices)
    width, plane_rows = block // CHUNKS, grp_count * rows
    bf16, f32 = jnp.bfloat16, jnp.float32
    roles = capacity + 1
    in_length, out_length = LISTS[level]
    vmem, hbm = pl.BlockSpec(memory_space=pltpu.VMEM), pl.BlockSpec(memory_space=pl.ANY)
    return pl.pallas_call(
        functools.partial(step_kernel, sizes, LISTS[level]),
        out_shape=(
            jax.ShapeDtypeStruct(stats_left.shape, f32),
            jax.ShapeDtypeStruct(stats_right.shape, f32),
            jax.ShapeDtypeStruct(grad.shape, bf16),
        ),
        in_specs=[vmem] * 2 + [hbm] * 5,
        out_specs=(hbm, hbm, vmem),
        scratch_shapes=[
            pltpu.VMEM((matrices * (total_width // block), rows, block), bf16),
            pltpu.VMEM((CHUNKS, grp_count, in_length, rows, width), bf16),
            [pltpu.VMEM((grp_count * in_length, rows, width), bf16)] * CHUNKS,
            pltpu.VMEM((CHUNKS, fsdp_count * roles, plane_rows, width), bf16),
            pltpu.VMEM((roles, block, block), bf16),
            pltpu.VMEM((roles, block, block), f32),
            pltpu.VMEM((roles, block, block), bf16),
            pltpu.VMEM((CHUNKS, block, width), bf16),
            pltpu.VMEM((capacity, block, block), bf16),
            [pltpu.VMEM((fsdp_count * capacity, plane_rows, width), bf16)] * CHUNKS,
            pltpu.VMEM((CHUNKS, grp_count, out_length, rows, width), bf16),
            [pltpu.VMEM((grp_count * out_length, rows, width), bf16)] * CHUNKS,
            pltpu.VMEM((roles, 2, block, block), bf16),
            pltpu.VMEM(stats_left.shape, f32),
            pltpu.VMEM(stats_right.shape, f32),
            pltpu.VMEM((8, 512), jnp.int32),
            pltpu.SMEM((8, 512), jnp.int32),
            pltpu.SemaphoreType.DMA((7,)),
            pltpu.SemaphoreType.DMA((4, CHUNKS)),
            pltpu.SemaphoreType.DMA((5, CHUNKS)),
            pltpu.SemaphoreType.DMA((5, CHUNKS)),
        ],
        compiler_params=pltpu.CompilerParams(
            collective_id=1 + level, has_side_effects=True, vmem_limit_bytes=28 * 1024 * 1024
        ),
        name="listed_step",
    )(owner[None], refresh[None], grad, stats_left, stats_right, old_roots, fresh_roots)


def hand_over_kernel(pieces, *refs):
    count = len(refs) // 3
    into, out_of = refs[-2:]
    moves = []
    for n in range(count):
        source, target, room = refs[n], refs[count + n], refs[2 * count + n]
        share = source.shape[0] // pieces
        for p in range(pieces):
            some, i = pl.ds(p * share, share), n * pieces + p
            moves.append(
                (
                    pltpu.make_async_copy(source.at[some], room.at[some], into.at[i]),
                    pltpu.make_async_copy(room.at[some], target.at[some], out_of.at[i]),
                )
            )
    for fetch, _ in moves:
        fetch.start()
    for fetch, store in moves:
        fetch.wait()
        store.start()
    for _, store in moves:
        store.wait()


def hand_over(*arrays):
    pieces = 2
    hbm = pl.BlockSpec(memory_space=pl.ANY)
    sems = pltpu.SemaphoreType.DMA((len(arrays) * pieces,))
    return pl.pallas_call(
        functools.partial(hand_over_kernel, pieces),
        out_shape=[jax.ShapeDtypeStruct(a.shape, a.dtype) for a in arrays],
        in_specs=[hbm] * len(arrays),
        out_specs=[hbm] * len(arrays),
        scratch_shapes=[pltpu.VMEM(a.shape, a.dtype) for a in arrays] + [sems, sems],
        compiler_params=pltpu.CompilerParams(vmem_limit_bytes=16 * 1024 * 1024),
        name="hand_over",
    )(*arrays)


def local(*arrays):
    grad, owner, refresh, *held = arrays
    branch = too_short(owner, refresh, lax.axis_size("grp"), held[0].shape[0])
    plans = [
        lambda level=level: listed_plan(level, owner, refresh, grad, *held) for level in range(len(LISTS))
    ]
    return tuple(hand_over(*lax.switch(branch, [*plans, lambda: dense_plan(*arrays)])))


def solution(mesh):
    return jax.shard_map(
        local,
        mesh=mesh,
        in_specs=(
            P(None, ("fsdp", "grp"), None),
            P(),
            P(),
            P(("fsdp", "grp"), None, None),
            P(("fsdp", "grp"), None, None),
            P(("fsdp", "grp"), None, None, None),
            P(("fsdp", "grp"), None, None, None),
        ),
        out_specs=(
            P(("fsdp", "grp"), None, None),
            P(("fsdp", "grp"), None, None),
            P(None, ("fsdp", "grp"), None),
        ),
        check_vma=False,
    )
```
